32 devices in a mesh: copy: 8 (over z, y), head: 4 (over x, core).
Axes of the slice: x: 2, y: 2, z: 4, core: 2. Of those that a mesh axis runs over, the one named last changes fastest.
Arguments:
- query: bfloat16 [8, 16, 48, 512], P('copy', 'head'), may hold values from -6 to 6
- keys: bfloat16 [8, 16, 48, 512], P('copy', 'head'), may hold values from -6 to 6
- values: bfloat16 [8, 16, 48, 512], P('copy', 'head'), may hold values from -6 to 6
- d_gated: bfloat16 [8, 16, 48, 512], P('copy', 'head'), may hold values from -48 to 48
- tokens: bfloat16 [8, 512, 768], P('copy', 'head'), may hold values from -6 to 6
- projections: bfloat16 [4, 16, 48, 768], P(None, 'head'), may hold values from -0.21875 to 0.21875
- pair_bias: bfloat16 [16, 512, 512], P('head'), may hold values from -6 to 6
- pair: bfloat16 [512, 512, 128], P('head', 'copy'), may hold values from -6 to 6
- bias_weight: bfloat16 [128, 16], replicated, may hold values from -1.5 to 1.5
- atom_mask: int32 [512], replicated, may hold values 0 or 1
- token_offsets: int32 [512], replicated, may hold values from 0 to 1536, as said below
Outputs:
- d_tokens: bfloat16 [8, 512, 768], P('copy', 'head')
- d_projections: float32 [4, 16, 48, 768], P(None, 'head')
- d_pair: bfloat16 [512, 512, 128], P('head', 'copy')
- d_bias_weight: float32 [128, 16], replicated
- d_rel_table: float32 [16, 65], replicated
The draws below stay inside these ranges and needn't reach their ends.
Inputs may be any that keep to these rules, and one draw needn't show every extreme that they name: `token_offsets`: never decreasing along the window, 0 at its first token and 1536 at its last; neighbouring tokens may share a value, and chain breaks leave gaps.
All inputs are finite; a program needn't handle non-finite values.
Results may differ from the reference program's by a relative error of at most 0.025.
Values may be sent and summed in bfloat16 or wider, within the bound.
A program may use at most 64 MiB of HBM per device.

```python
import math
import jax
import jax.numpy as jnp
from jax import lax

D = 768
HEADS = 16
HD = 48
CP = 128
BINS = 65
TOKENS = 512
COPIES = 8
HEAD_GROUP = 4
N_HEAD = 4


def paired_draw(key):
    shape = (COPIES, HEADS, HD, TOKENS)
    base = jax.random.fold_in(key, 4099)
    split_keys = jax.random.split(base, 2)
    queries = jnp.clip(jax.random.normal(split_keys[0], shape, jnp.float32), -6.0, 6.0)
    keyset = jnp.clip(jax.random.normal(split_keys[1], shape, jnp.float32), -6.0, 6.0)
    return (queries, keyset)


def draw_query(key, part):
    return paired_draw(key)[0].astype(jnp.bfloat16)


def draw_keys(key, part):
    return paired_draw(key)[1].astype(jnp.bfloat16)


def draw_token_offsets(key, part):
    base = jax.random.fold_in(key, 77)
    step_key, jump_key = jax.random.split(base)
    increments = jax.random.randint(step_key, (TOKENS,), 0, 3)
    jumps = jnp.where(jax.random.randint(jump_key, (TOKENS,), 0, 64) == 0, 40, 0)
    increments = (increments + jumps).at[0].set(0)
    running = jnp.minimum(jnp.cumsum(increments), 3 * TOKENS - 1)
    return running.at[TOKENS - 1].set(3 * TOKENS).astype(jnp.int32)


def place_ends(values, own_key, least, high):
    extent = values.shape
    index_at = [jax.random.randint(jax.random.fold_in(own_key, axis), (), 0, extent[axis]) for axis in range(len(extent))]
    values = values.at[tuple(index_at)].set(least)
    longest = extent.index(max(extent))
    index_at[longest] = (index_at[longest] + 1) % extent[longest]
    return values.at[tuple(index_at)].set(high)


def levels(own_key, dims, pieces, smallest, largest):
    def one(axis_at, blocks):
        draws = jax.random.uniform(jax.random.fold_in(jax.random.fold_in(own_key, 6), axis_at), (blocks,), jnp.float32, smallest / len(pieces), largest / len(pieces))
        return jnp.repeat(jnp.exp(draws), dims[axis_at] // blocks).reshape((-1,) + (1,) * (len(dims) - axis_at - 1))

    factor_of = one(*pieces[0])
    for cut in pieces[1:]:
        factor_of = factor_of * one(*cut)
    return factor_of


def centred(stream_key, extent, spread, most, pieces=(), held_as=jnp.bfloat16):
    result = jax.random.normal(stream_key, extent, jnp.float32) * spread
    if len(pieces) > 0:
        result = levels(stream_key, extent, pieces, -0.22, 0.18) * result
    return jnp.clip(result, min=-most, max=most).astype(held_as)


def setup_inputs(seed: int = 0) -> dict:
    arg_keys = jax.random.split(jax.random.key(seed), 12)
    query = draw_query(jax.random.fold_in(arg_keys[11], 71), 0)
    keys = draw_keys(jax.random.fold_in(arg_keys[11], 71), 0)
    values = centred(arg_keys[2], (COPIES, HEADS, HD, TOKENS), 1.0, 6.0, ((0, 8), (1, 4)))
    d_gated = centred(arg_keys[3], (COPIES, HEADS, HD, TOKENS), 8.0, 48.0, ((0, 8), (1, 4)))
    tokens = centred(arg_keys[4], (COPIES, TOKENS, D), 1.0, 6.0, ((0, 8), (1, 4)))
    projections = centred(arg_keys[5], (4, HEADS, HD, D), D ** -0.5, 0.21875, ((1, 4),))
    pair_bias = centred(arg_keys[6], (HEADS, TOKENS, TOKENS), 1.0, 6.0, ((0, 4),))
    pair = centred(arg_keys[7], (TOKENS, TOKENS, CP), 1.0, 6.0, ((0, 4), (1, 8)))
    bias_weight = centred(arg_keys[8], (CP, HEADS), HEADS ** -0.5, 1.5)
    atom_mask = place_ends((jax.random.randint(arg_keys[9], (TOKENS,), 0, 8) < 7).astype(jnp.int32), jax.random.fold_in(arg_keys[9], 1), 0, 1)
    token_offsets = draw_token_offsets(jax.random.fold_in(arg_keys[11], 71), 0)
    return dict(query=query, keys=keys, values=values, d_gated=d_gated, tokens=tokens, projections=projections, pair_bias=pair_bias, pair=pair, bias_weight=bias_weight, atom_mask=atom_mask, token_offsets=token_offsets)


MASKED_SCORE = -1000000000.0

def head_backward(query, keys, values, d_gated, bias, gate_pre, key_valid):
    score_scale = 1.0 / math.sqrt(HD)
    scores = jnp.dot(query.T, keys, preferred_element_type=jnp.float32) * score_scale + bias.astype(jnp.float32)
    scores = jnp.where(key_valid[None, :], scores, MASKED_SCORE)
    row_peak = lax.optimization_barrier(jnp.max(scores, axis=1, keepdims=True))
    exponent = jnp.exp(scores - row_peak)
    soft_probs = exponent / lax.optimization_barrier(jnp.sum(exponent, axis=1, keepdims=True))
    weights = soft_probs.astype(jnp.bfloat16)
    attended = jnp.dot(values, weights.T, preferred_element_type=jnp.float32)
    gate_open = jax.nn.sigmoid(gate_pre)
    upstream = d_gated.astype(jnp.float32)
    d_attended = (upstream * gate_open).astype(jnp.bfloat16)
    d_gate = (upstream * attended * gate_open * (1.0 - gate_open)).astype(jnp.bfloat16)
    d_probs = jnp.dot(d_attended.T, values, preferred_element_type=jnp.float32)
    d_scores = (soft_probs * (d_probs - lax.optimization_barrier(jnp.sum(soft_probs * d_probs, axis=1, keepdims=True)))).astype(jnp.bfloat16)
    d_values = jnp.dot(d_attended, weights, preferred_element_type=jnp.float32).astype(jnp.bfloat16)
    d_query = (jnp.dot(keys, d_scores.T, preferred_element_type=jnp.float32) * score_scale).astype(jnp.bfloat16)
    d_keys = (jnp.dot(query, d_scores, preferred_element_type=jnp.float32) * score_scale).astype(jnp.bfloat16)
    return (jnp.stack([d_query, d_keys, d_values, d_gate]), d_scores)

def reference(query, keys, values, d_gated, tokens, projections, pair_bias, pair, bias_weight, atom_mask, token_offsets):
    key_valid = atom_mask > 0
    proj_f = projections.astype(jnp.float32)

    def per_copy(totals, inputs):
        bias_total, proj_total = totals
        copy_query, copy_keys, copy_values, copy_upstream, copy_tokens = inputs
        tokens_f = copy_tokens.astype(jnp.float32)
        gate_pre = jnp.einsum('id,hkd->hki', tokens_f, proj_f[3])

        def per_head(arrays):
            return head_backward(arrays[0], arrays[1], arrays[2], arrays[3], arrays[4], arrays[5], key_valid)
        head_cots, d_scores = lax.map(per_head, (copy_query, copy_keys, copy_values, copy_upstream, pair_bias, gate_pre))
        cotangents = jnp.transpose(head_cots, (1, 0, 2, 3)).astype(jnp.float32)
        proj_total = proj_total + jnp.einsum('mhki,id->mhkd', cotangents, tokens_f)
        head_terms = jnp.einsum('mhki,mhkd->hid', cotangents, proj_f)
        grouped = lax.optimization_barrier(jnp.sum(head_terms.reshape(HEADS // HEAD_GROUP, HEAD_GROUP, TOKENS, D), axis=1)).astype(jnp.bfloat16)
        grouped = lax.optimization_barrier(grouped)
        copy_grad = lax.optimization_barrier(jnp.sum(grouped.astype(jnp.float32), axis=0)).astype(jnp.bfloat16)
        bias_total = bias_total + d_scores.astype(jnp.float32)
        return ((bias_total, proj_total), copy_grad)
    start_totals = (jnp.zeros((HEADS, TOKENS, TOKENS), jnp.float32), jnp.zeros((4, HEADS, HD, D), jnp.float32))
    (bias_total, d_projections), d_tokens = lax.scan(per_copy, start_totals, (query, keys, values, d_gated, tokens))
    d_bias = bias_total.astype(jnp.bfloat16)
    row_block = TOKENS // N_HEAD
    reach_bins = (BINS - 1) // 2
    bias_blocks = jnp.transpose(d_bias.reshape(HEADS, N_HEAD, row_block, TOKENS), (1, 0, 2, 3))
    pair_blocks = pair.reshape(N_HEAD, row_block, TOKENS, CP)
    offset_blocks = token_offsets.reshape(N_HEAD, row_block)
    weight_f = bias_weight.astype(jnp.float32)

    def per_block(arrays):
        block_bias, block_pair, block_offsets = arrays
        bias_f = block_bias.astype(jnp.float32)
        pair_grad = jnp.einsum('hij,ch->ijc', bias_f, weight_f).astype(jnp.bfloat16)
        weight_part = jnp.einsum('ijc,hij->ch', block_pair.astype(jnp.float32), bias_f)
        bin_index = jnp.clip(token_offsets[None, :] - block_offsets[:, None], -reach_bins, reach_bins) + reach_bins
        one_hot = (bin_index[:, :, None] == jnp.arange(BINS, dtype=jnp.int32)[None, None, :]).astype(jnp.float32)
        table_part = jnp.einsum('hij,ijb->hb', bias_f, one_hot)
        return (pair_grad, weight_part, table_part)
    pair_grads, weight_parts, table_parts = lax.map(per_block, (bias_blocks, pair_blocks, offset_blocks))
    d_pair = pair_grads.reshape(TOKENS, TOKENS, CP)
    d_bias_weight = lax.optimization_barrier(jnp.sum(weight_parts, axis=0))
    d_rel_table = lax.optimization_barrier(jnp.sum(table_parts, axis=0))
    return (d_tokens, d_projections, d_pair, d_bias_weight, d_rel_table)
```

```python
import functools
import math

import jax
import jax.numpy as jnp
from jax import lax
from jax.experimental import pallas as pl
from jax.experimental.pallas import tpu as pltpu
from jax.sharding import PartitionSpec as P

BINS = 65
MASKED_SCORE = -1000000000.0
MESH = pl.DeviceIdType.MESH
F32 = jnp.float32
BF16 = jnp.bfloat16


def contract(a, b, da, db):
    return lax.dot_general(a, b, (((da,), (db,)), ((), ())), preferred_element_type=F32)


def bit_of(index, b):
    return (index // (1 << b)) % 2


def flip(index, b):
    return index + (1 - 2 * bit_of(index, b)) * (1 << b)


def rest(count):
    return (slice(None),) * count


def main_kernel(
    n, nh, scale,
    q_ref, k_ref, v_ref, dg_ref, own_ref, proj_ref, bias_ref, mask_ref,
    dtok_out, dproj_out, dbias_out,
    tok, bt, gate, w_s, ds, cot, dp, pg, dt, sb, rs, ps, ts,
    tok_sem, ds_sem, dp_sem, pg_sem, dt_sem, sb_sem,
):
    lc, lh = n.bit_length() - 1, nh.bit_length() - 1
    heads, hd, t = q_ref.shape
    d = own_ref.shape[1]
    rows = 4 * heads * hd
    tr = t // nh
    j = t // n
    copy = lax.axis_index("copy")
    head = lax.axis_index("head")
    cb = [bit_of(copy, b) for b in range(lc)]
    hb = [bit_of(head, b) for b in range(lh)]

    barrier = pltpu.get_barrier_semaphore()
    for b in range(lc):
        pl.semaphore_signal(barrier, inc=1, device_id={"copy": flip(copy, b)}, device_id_type=MESH)
    for step in range(1, nh):
        pl.semaphore_signal(
            barrier, inc=1, device_id={"head": (head + step) % nh}, device_id_type=MESH
        )
    own_index = tuple(hb[b] for b in reversed(range(lh)))
    tok[own_index] = own_ref[...]
    pl.semaphore_wait(barrier, lc + nh - 1)

    def remote(src, dst, sems, index, device):
        return pltpu.make_async_remote_copy(
            src_ref=src,
            dst_ref=dst,
            send_sem=sems.at[(0,) + index],
            recv_sem=sems.at[(1,) + index],
            device_id=device,
            device_id_type=MESH,
        )

    def spread(ref, bits, b, sems, device):
        at = rest(len(bits) - 1 - b) + tuple(bits[x] for x in reversed(range(b + 1)))
        return remote(ref.at[at], ref.at[at], sems, (b,), device)

    def halve(src, dst, bits, s, sems, index, device, lead=()):
        at = lead + rest(len(bits) - s - 1) + (1 - bits[s],)
        to = dst.at[lead] if lead else dst
        return remote(src.at[at], to, sems, index, device)

    def fold(src, dst, bits, s, lead=()):
        at = lead + rest(len(bits) - s - 1) + (bits[s],)
        whole = lead if lead else Ellipsis
        dst[whole] = (src[at].astype(F32) + dst[whole].astype(F32)).astype(BF16)

    def tok_copy(b):
        return spread(tok, hb, b, tok_sem, {"head": flip(head, b)})

    def ds_copy(h, s):
        src = ds if s == 0 else rs[s - 1]
        return halve(src, rs[s], cb, s, ds_sem, (h, s), {"copy": flip(copy, s)}, (h,))

    def dp_copy(s):
        src = dp if s == 0 else ps[s - 1]
        return halve(src, ps[s], cb, s, dp_sem, (s,), {"copy": flip(copy, s)})

    def pg_copy(b):
        return spread(pg, cb, b, pg_sem, {"copy": flip(copy, b)})

    def dt_copy(s):
        src = dt if s == 0 else ts[s - 1]
        return halve(src, ts[s], hb, s, dt_sem, (s,), {"head": flip(head, s)})

    def sb_copy(step):
        peer = (head + step) % nh
        return remote(sb.at[peer], dbias_out.at[head], sb_sem, (step,), {"head": peer})

    tok_copy(lh - 1).start()

    @pl.loop(0, heads)
    def _(h):
        bt[h] = bias_ref[h].T

    for b in reversed(range(lh)):
        tok_copy(b).wait_recv()
        if b > 0:
            tok_copy(b - 1).start()
    tokens = tok[...].reshape(t, d)
    gate_pre = contract(proj_ref[3 * heads * hd :, :], tokens, 1, 1)
    gate[...] = jax.nn.sigmoid(gate_pre).reshape(heads, hd, t)

    ib = min(t, 256)

    def compute(h):
        valid = mask_ref[...] > 0
        keys, values = k_ref[h], v_ref[h]
        for start in range(0, t, ib):
            cols = pl.ds(start, ib)
            query = q_ref[h, :, cols]
            s = contract(keys, query, 0, 0) * scale + bt[h, :, cols].astype(F32)
            s = jnp.where(valid, s, MASKED_SCORE)
            e = jnp.exp(s - jnp.max(s, axis=0, keepdims=True))
            p = e * (1.0 / jnp.sum(e, axis=0, keepdims=True))
            w = p.astype(BF16)
            w_s[:, cols] = w
            att = contract(values, w, 1, 0)
            g = gate[h, :, cols]
            up = dg_ref[h, :, cols].astype(F32)
            datt = (up * g).astype(BF16)
            cot[2, h, :, cols] = datt
            cot[3, h, :, cols] = (up * att * g * (1.0 - g)).astype(BF16)
            inner = jnp.sum(datt.astype(F32) * att, axis=0, keepdims=True)
            dprob = contract(values, datt, 0, 0)
            dsb = (p * (dprob - inner)).astype(BF16)
            ds[(h,) + rest(lc + 1) + (cols,)] = dsb.reshape((2,) * lc + (j, ib))
            cot[0, h, :, cols] = (contract(keys, dsb, 1, 0) * scale).astype(BF16)

    def finish(h):
        full = ds[h].reshape(t, t)
        cot[1, h] = (contract(q_ref[h], full, 1, 1) * scale).astype(BF16)
        cot[2, h] = contract(cot[2, h], w_s[...], 1, 1).astype(BF16)

    def advance(h, s):
        ds_copy(h, s - 1).wait_recv()
        fold(ds if s == 1 else rs[s - 2], rs[s - 1], cb, s - 1, (h,))
        if s < lc:
            ds_copy(h, s).start()

    @pl.loop(0, heads)
    def _(h):
        compute(h)
        ds_copy(h, 0).start()
        finish(h)
        for s in range(1, lc + 1):

            @pl.when(h >= s)
            def _():
                advance(h - s, s)

    def drain(now):
        for s in range(1, lc + 1):
            if 0 <= now - s < heads:
                advance(now - s, s)

    flat = cot[...].reshape(rows, t)
    part = contract(flat, tok[...].reshape(t, d), 1, 0).astype(BF16)
    sr = dp.shape[-2]
    if rows < n * sr:
        part = jnp.concatenate([part, jnp.zeros((n * sr - rows, d), BF16)], axis=0)
    dp[...] = part.reshape((2,) * lc + (sr, d))
    dp_copy(0).start()
    drain(heads)
    dt[...] = contract(flat, proj_ref[...], 0, 0).astype(BF16).reshape((2,) * lh + (tr, d))
    dt_copy(0).start()
    for now in range(heads + 1, heads + lc):
        drain(now)

    total = rs[lc - 1]
    for peer in range(nh):
        sb[peer] = total[:, :, peer * tr : (peer + 1) * tr]
    for step in range(1, nh):
        sb_copy(step).start()
    dbias_out[head] = sb[head]

    def dp_advance(s):
        dp_copy(s - 1).wait_recv()
        fold(dp if s == 1 else ps[s - 2], ps[s - 1], cb, s - 1)
        if s < lc:
            dp_copy(s).start()

    dp_advance(1)
    for s in range(1, lh + 1):
        dt_copy(s - 1).wait_recv()
        fold(dt if s == 1 else ts[s - 2], ts[s - 1], hb, s - 1)
        if s < lh:
            dt_copy(s).start()
        if s + 1 <= lc:
            dp_advance(s + 1)
    for s in range(lh + 2, lc + 1):
        dp_advance(s)
    dtok_out[...] = ts[lh - 1][...]
    pg[tuple(cb[b] for b in reversed(range(lc)))] = ps[lc - 1][...]
    for b in reversed(range(lc)):
        pg_copy(b).start()
        pg_copy(b).wait_recv()
    dproj_out[...] = pg[...].reshape(n * sr, d)[:rows].astype(F32)
    for step in range(1, nh):
        sb_copy(step).wait()
    for b in range(lh):
        tok_copy(b).wait_send()
        dt_copy(b).wait_send()
    for b in range(lc):
        dp_copy(b).wait_send()
        pg_copy(b).wait_send()

    @pl.loop(0, heads)
    def _(h):
        for s in range(lc):
            ds_copy(h, s).wait_send()


def sum_kernel(n, nh, x_ref, o_ref, first, second, sem_a, sem_b):
    copy = lax.axis_index("copy")
    head = lax.axis_index("head")
    barrier = pltpu.get_barrier_semaphore()
    for step in range(1, n):
        pl.semaphore_signal(
            barrier, inc=1, device_id={"copy": (copy + step) % n}, device_id_type=MESH
        )
    for step in range(1, nh):
        pl.semaphore_signal(
            barrier, inc=1, device_id={"head": (head + step) % nh}, device_id_type=MESH
        )
    first[copy] = x_ref[...]
    pl.semaphore_wait(barrier, n + nh - 2)

    def exchange(buf, me, count, sems, axis):
        def make(step):
            return pltpu.make_async_remote_copy(
                src_ref=buf.at[me],
                dst_ref=buf.at[me],
                send_sem=sems.at[0, step],
                recv_sem=sems.at[1, step],
                device_id={axis: (me + step) % count},
                device_id_type=MESH,
            )

        for step in range(1, count):
            make(step).start()
        for step in range(1, count):
            make(step).wait()
        total = buf[0]
        for index in range(1, count):
            total = total + buf[index]
        return total

    second[head] = exchange(first, copy, n, sem_a, "copy")
    o_ref[...] = exchange(second, head, nh, sem_b, "head")


def vmem():
    return pl.BlockSpec(memory_space=pltpu.VMEM)


def shards(
    n, nh, query, keys, values, d_gated, tokens, projections, pair_bias, pair, bias_weight,
    atom_mask, token_offsets,
):
    heads, hd, t = query.shape[1:]
    d = tokens.shape[2]
    lc, lh = n.bit_length() - 1, nh.bit_length() - 1
    rows = 4 * heads * hd
    tr, j = t // nh, t // n
    sr = -(-rows // (n * 16)) * 16
    args = (
        query[0], keys[0], values[0], d_gated[0], tokens[0], projections.reshape(rows, d),
        pair_bias, atom_mask.reshape(t, 1),
    )
    dma = pltpu.SemaphoreType.DMA
    d_tokens, d_proj, d_bias = pl.pallas_call(
        functools.partial(main_kernel, n, nh, 1.0 / math.sqrt(hd)),
        out_shape=(
            jax.ShapeDtypeStruct((tr, d), BF16),
            jax.ShapeDtypeStruct((rows, d), F32),
            jax.ShapeDtypeStruct((nh, heads, j, tr), BF16),
        ),
        in_specs=[vmem()] * len(args),
        out_specs=(vmem(),) * 3,
        scratch_shapes=[
            pltpu.VMEM((2,) * lh + (tr, d), BF16),
            pltpu.VMEM((heads, t, t), BF16),
            pltpu.VMEM((heads, hd, t), F32),
            pltpu.VMEM((t, t), BF16),
            pltpu.VMEM((heads,) + (2,) * lc + (j, t), BF16),
            pltpu.VMEM((4, heads, hd, t), BF16),
            pltpu.VMEM((2,) * lc + (sr, d), BF16),
            pltpu.VMEM((2,) * lc + (sr, d), BF16),
            pltpu.VMEM((2,) * lh + (tr, d), BF16),
            pltpu.VMEM((nh, heads, j, tr), BF16),
            [pltpu.VMEM((heads,) + (2,) * (lc - s - 1) + (j, t), BF16) for s in range(lc)],
            [pltpu.VMEM((2,) * (lc - s - 1) + (sr, d), BF16) for s in range(lc)],
            [pltpu.VMEM((2,) * (lh - s - 1) + (tr, d), BF16) for s in range(lh)],
            dma((2, lh)), dma((2, heads, lc)), dma((2, lc)), dma((2, lc)), dma((2, lh)),
            dma((2, nh)),
        ],
        compiler_params=pltpu.CompilerParams(
            collective_id=0, has_side_effects=True, vmem_limit_bytes=48 * 2**20
        ),
    )(*args)
    d_bias = d_bias.reshape(nh * heads, j, tr)
    d_pair = jnp.einsum("hji,ch->ijc", d_bias, bias_weight, preferred_element_type=F32).astype(BF16)
    weight_part = jnp.einsum("ijc,hji->hc", pair, d_bias, preferred_element_type=F32)
    row_offsets = lax.dynamic_slice_in_dim(token_offsets, lax.axis_index("head") * tr, tr)
    col_offsets = lax.dynamic_slice_in_dim(token_offsets, lax.axis_index("copy") * j, j)
    reach = (BINS - 1) // 2
    bin_index = jnp.clip(col_offsets[:, None] - row_offsets[None, :], -reach, reach) + reach
    one_hot = (bin_index[:, :, None] == jnp.arange(BINS, dtype=jnp.int32)[None, None, :]).astype(
        BF16
    )
    table_part = jnp.einsum("hji,jib->hb", d_bias, one_hot, preferred_element_type=F32)
    wide = -(-BINS // 128) * 128
    both = jnp.concatenate([weight_part, jnp.pad(table_part, ((0, 0), (0, wide - BINS)))], axis=1)
    summed = pl.pallas_call(
        functools.partial(sum_kernel, n, nh),
        out_shape=jax.ShapeDtypeStruct(both.shape, F32),
        in_specs=[vmem()],
        out_specs=vmem(),
        scratch_shapes=[
            pltpu.VMEM((n,) + both.shape, F32),
            pltpu.VMEM((nh,) + both.shape, F32),
            dma((2, n)),
            dma((2, nh)),
        ],
        compiler_params=pltpu.CompilerParams(collective_id=1, has_side_effects=True),
    )(both)
    channels = bias_weight.shape[0]
    return (
        d_tokens[None],
        d_proj.reshape(projections.shape),
        d_pair,
        summed[:, :channels].T,
        summed[:, channels : channels + BINS],
    )


def solution(mesh):
    in_specs = (
        P("copy", "head", None, None),
        P("copy", "head", None, None),
        P("copy", "head", None, None),
        P("copy", "head", None, None),
        P("copy", "head", None),
        P(None, "head", None, None),
        P("head", None, None),
        P("head", "copy", None),
        P(),
        P(),
        P(),
    )
    out_specs = (
        P("copy", "head", None),
        P(None, "head", None, None),
        P("head", "copy", None),
        P(),
        P(),
    )
    body = functools.partial(shards, mesh.shape["copy"], mesh.shape["head"])
    return jax.shard_map(body, mesh=mesh, in_specs=in_specs, out_specs=out_specs, check_vma=False)
```

```python
import functools
import math

import jax
import jax.numpy as jnp
from jax import lax
from jax.experimental import pallas as pl
from jax.experimental.pallas import tpu as pltpu
from jax.sharding import PartitionSpec as P

BINS = 65
MASKED_SCORE = -1000000000.0
MESH = pl.DeviceIdType.MESH
F32 = jnp.float32
BF16 = jnp.bfloat16


def contract(a, b, da, db):
    return lax.dot_general(a, b, (((da,), (db,)), ((), ())), preferred_element_type=F32)


def bit_of(index, b):
    return (index // (1 << b)) % 2


def flip(index, b):
    return index + (1 - 2 * bit_of(index, b)) * (1 << b)


def rest(count):
    return (slice(None),) * count


def main_kernel(
    n, nh, scale,
    off_ref, q_hbm, k_hbm, v_hbm, dg_hbm, own_hbm, proj_hbm, bias_hbm, pair_hbm, bw_ref, mask_ref,
    offrow_ref,
    dtok_out, dproj_out, dpair_out, sums_out,
    q_ref, k_ref, v_ref, dg_ref, proj_ref, bias_ref, pair_ref,
    valid_s, off_s, tok, bt, gate, w_s, ds, cot, dt, sb, rb, xs, first, second, dp, pg, rs, ps, ts,
    in_sem, tok_sem, ds_sem, dp_sem, pg_sem, dt_sem, sb_sem, first_sem, second_sem,
):
    lc, lh = n.bit_length() - 1, nh.bit_length() - 1
    heads, hd, t = q_ref.shape
    d = own_hbm.shape[1]
    rows = 4 * heads * hd
    tr = t // nh
    j = t // n
    halves = len(dp)
    dh = d // halves
    copy = lax.axis_index("copy")
    head = lax.axis_index("head")
    cb = [bit_of(copy, b) for b in range(lc)]
    hb = [bit_of(head, b) for b in range(lh)]
    up_order = tuple(range(lc))
    orders = (up_order[1:] + up_order[:1], up_order)

    barrier = pltpu.get_barrier_semaphore()
    for step in range(1, n):
        pl.semaphore_signal(
            barrier, inc=1, device_id={"copy": (copy + step) % n}, device_id_type=MESH
        )
    for step in range(1, nh):
        pl.semaphore_signal(
            barrier, inc=1, device_id={"head": (head + step) % nh}, device_id_type=MESH
        )
    own_index = tuple(hb[b] for b in reversed(range(lh)))
    loads = [
        pltpu.make_async_copy(src, dst, in_sem.at[index])
        for index, (src, dst) in enumerate((
            (own_hbm, tok.at[own_index]), (bias_hbm, bias_ref), (proj_hbm, proj_ref),
            (q_hbm, q_ref), (k_hbm, k_ref), (v_hbm, v_ref), (dg_hbm, dg_ref),
            (pair_hbm, pair_ref),
        ))
    ]
    for load in loads:
        load.start()

    def remote(src, dst, sems, index, device):
        return pltpu.make_async_remote_copy(
            src_ref=src,
            dst_ref=dst,
            send_sem=sems.at[(0,) + index],
            recv_sem=sems.at[(1,) + index],
            device_id=device,
            device_id_type=MESH,
        )

    def pick(order, bits, s, other):
        left = sorted(order[s:], reverse=True)
        bit = bits[order[s]]
        return rest(left.index(order[s])) + ((1 - bit if other else bit),)

    def halve(src, dst, order, bits, s, sems, index, device, lead=()):
        to = dst.at[lead] if lead else dst
        return remote(src.at[lead + pick(order, bits, s, True)], to, sems, index, device)

    def fold(src, dst, order, bits, s, lead=()):
        whole = lead if lead else Ellipsis
        mine = src[lead + pick(order, bits, s, False)]
        dst[whole] = (mine.astype(F32) + dst[whole].astype(F32)).astype(BF16)

    def spread(ref, order, bits, s, sems, index, device):
        done = order[s + 1 :]
        at = tuple(
            slice(None) if b in done else bits[b] for b in reversed(range(len(bits)))
        )
        return remote(ref.at[at], ref.at[at], sems, index, device)

    def tok_copy(b):
        return spread(tok, tuple(range(lh)), hb, b, tok_sem, (b,), {"head": flip(head, b)})

    def ds_copy(h, s):
        src = ds if s == 0 else rs[s - 1]
        return halve(
            src, rs[s], up_order, cb, s, ds_sem, (h, s), {"copy": flip(copy, s)}, (h,)
        )

    def dp_copy(c, s):
        src = dp[c] if s == 0 else ps[c][s - 1]
        device = {"copy": flip(copy, orders[c][s])}
        return halve(src, ps[c][s], orders[c], cb, s, dp_sem, (c, s), device)

    def pg_copy(c, s):
        device = {"copy": flip(copy, orders[c][s])}
        return spread(pg[c], orders[c], cb, s, pg_sem, (c, s), device)

    def dt_copy(s):
        src = dt if s == 0 else ts[s - 1]
        return halve(
            src, ts[s], tuple(range(lh)), hb, s, dt_sem, (s,), {"head": flip(head, s)}
        )

    def sb_copy(step):
        peer = (head + step) % nh
        return remote(sb.at[peer], rb.at[head], sb_sem, (step,), {"head": peer})

    def first_copy(step):
        here = first.at[copy]
        return remote(here, here, first_sem, (step,), {"copy": (copy + step) % n})

    def second_copy(step):
        here = second.at[head]
        return remote(here, here, second_sem, (step,), {"head": (head + step) % nh})

    loads[0].wait()
    pl.semaphore_wait(barrier, n + nh - 2)
    tok_copy(lh - 1).start()
    wide = valid_s.shape[1]
    valid_s[...] = jnp.broadcast_to(mask_ref[...].astype(F32), (wide, t)).T
    off_s[...] = jnp.broadcast_to(offrow_ref[...].astype(F32), (wide, t)).T
    loads[1].wait()

    @pl.loop(0, heads)
    def _(h):
        bt[h] = bias_ref[h].T

    for b in reversed(range(lh)):
        tok_copy(b).wait_recv()
        if b > 0:
            tok_copy(b - 1).start()
    for load in loads[2:]:
        load.wait()
    tokens = tok[...].reshape(t, d)
    gate_pre = contract(proj_ref[3 * heads * hd :, :], tokens, 1, 1)
    gate[...] = jax.nn.sigmoid(gate_pre).reshape(heads, hd, t)

    ib = min(t, 256)

    def compute(h):
        valid = valid_s[:, 0:1] > 0.5
        keys, values = k_ref[h], v_ref[h]
        for start in range(0, t, ib):
            cols = pl.ds(start, ib)
            query = q_ref[h, :, cols]
            s = contract(keys, query, 0, 0) * scale + bt[h, :, cols].astype(F32)
            s = jnp.where(valid, s, MASKED_SCORE)
            e = jnp.exp(s - jnp.max(s, axis=0, keepdims=True))
            p = e * (1.0 / jnp.sum(e, axis=0, keepdims=True))
            w = p.astype(BF16)
            w_s[:, cols] = w
            att = contract(values, w, 1, 0)
            g = gate[h, :, cols]
            up = dg_ref[h, :, cols].astype(F32)
            datt = (up * g).astype(BF16)
            cot[2, h, :, cols] = datt
            cot[3, h, :, cols] = (up * att * g * (1.0 - g)).astype(BF16)
            inner = jnp.sum(datt.astype(F32) * att, axis=0, keepdims=True)
            dprob = contract(values, datt, 0, 0)
            dsb = (p * (dprob - inner)).astype(BF16)
            ds[(h,) + rest(lc + 1) + (cols,)] = dsb.reshape((2,) * lc + (j, ib))
            cot[0, h, :, cols] = (contract(keys, dsb, 1, 0) * scale).astype(BF16)

    def finish(h):
        full = ds[h].reshape(t, t)
        cot[1, h] = (contract(q_ref[h], full, 1, 1) * scale).astype(BF16)
        cot[2, h] = contract(cot[2, h], w_s[...], 1, 1).astype(BF16)

    def advance(h, s):
        ds_copy(h, s - 1).wait_recv()
        fold(ds if s == 1 else rs[s - 2], rs[s - 1], up_order, cb, s - 1, (h,))
        if s < lc:
            ds_copy(h, s).start()

    @pl.loop(0, heads)
    def _(h):
        compute(h)
        ds_copy(h, 0).start()
        finish(h)
        for s in range(1, lc + 1):

            @pl.when(h >= s)
            def _():
                advance(h - s, s)

    def drain(now):
        for s in range(1, lc + 1):
            if 0 <= now - s < heads:
                advance(now - s, s)

    def dp_advance(c, s):
        dp_copy(c, s - 1).wait_recv()
        fold(dp[c] if s == 1 else ps[c][s - 2], ps[c][s - 1], orders[c], cb, s - 1)
        if s < lc:
            dp_copy(c, s).start()

    def dt_advance(s):
        dt_copy(s - 1).wait_recv()
        fold(dt if s == 1 else ts[s - 2], ts[s - 1], tuple(range(lh)), hb, s - 1)
        if s < lh:
            dt_copy(s).start()

    flat = cot[...].reshape(rows, t)
    sr = dp[0].shape[-2]
    for c in range(halves):
        tokens = tok[...].reshape(t, d)[:, c * dh : (c + 1) * dh]
        part = contract(flat, tokens, 1, 0).astype(BF16)
        if rows < n * sr:
            part = jnp.concatenate([part, jnp.zeros((n * sr - rows, dh), BF16)], axis=0)
        dp[c][...] = part.reshape((2,) * lc + (sr, dh))
        dp_copy(c, 0).start()
    drain(heads)
    dt[...] = contract(flat, proj_ref[...], 0, 0).astype(BF16).reshape((2,) * lh + (tr, d))
    dt_copy(0).start()
    drain(heads + 1)
    dp_advance(0, 1)
    for now in range(heads + 2, heads + lc):
        drain(now)

    total = rs[lc - 1]
    for peer in range(nh):
        sb[peer] = total[:, :, peer * tr : (peer + 1) * tr]
    for step in range(1, nh):
        sb_copy(step).start()
    rb[head] = sb[head]

    for s in range(1, lc):
        if s <= lh:
            dt_advance(s)
        dp_advance(1, s)
        dp_advance(0, s + 1)
    for s in range(lc, lh + 1):
        dt_advance(s)
    dtok_out[...] = ts[lh - 1][...]
    mine = tuple(cb[b] for b in reversed(range(lc)))
    pg[0][mine] = ps[0][lc - 1][...]
    pg_copy(0, lc - 1).start()
    dp_advance(1, lc)
    pg[1][mine] = ps[1][lc - 1][...]
    pg_copy(1, lc - 1).start()

    def pg_advance(s):
        for c in range(halves):
            pg_copy(c, s).wait_recv()
            if s > 0:
                pg_copy(c, s - 1).start()

    for step in range(1, nh):
        sb_copy(step).wait()
    for peer in range(nh):
        for h in range(heads):
            xs[:, peer * heads + h, :] = rb[peer, h].astype(F32).T
    columns = off_s[pl.ds(pl.multiple_of(copy * j, j), j), :]
    bins = lax.broadcasted_iota(jnp.int32, (j, wide), 1).astype(F32)
    reach = (BINS - 1) // 2
    group = 8
    channels = bw_ref.shape[0]

    def pairs(g, acc):
        for u in range(group):
            i = g * group + u
            x = xs[i].astype(BF16)
            dpair_out[i] = contract(x, bw_ref[...], 0, 1).astype(BF16)
            gap = columns - off_ref[head * tr + i].astype(F32)
            hot = jnp.clip(gap, -reach, reach) + reach == bins
            right = jnp.concatenate([pair_ref[i], hot.astype(F32).astype(BF16)], axis=1)
            acc = acc + contract(x, right, 1, 0)
        return acc

    acc = jnp.zeros((nh * heads, channels + wide), F32)
    acc = lax.fori_loop(0, tr // group // 2, pairs, acc)
    pg_advance(lc - 1)
    acc = lax.fori_loop(tr // group // 2, tr // group, pairs, acc)
    first[copy] = acc
    for step in range(1, n):
        first_copy(step).start()
    for s in reversed(range(1, lc - 1)):
        pg_advance(s)
    for step in range(1, n):
        first_copy(step).wait()
    acc = first[0]
    for index in range(1, n):
        acc = acc + first[index]
    second[head] = acc
    for step in range(1, nh):
        second_copy(step).start()
    pg_advance(0)
    for c in range(halves):
        dproj_out[:, c * dh : (c + 1) * dh] = pg[c][...].reshape(n * sr, dh)[:rows]
    for step in range(1, nh):
        second_copy(step).wait()
    acc = second[0]
    for index in range(1, nh):
        acc = acc + second[index]
    sums_out[...] = acc
    for b in range(lh):
        tok_copy(b).wait_send()
        dt_copy(b).wait_send()
    for c in range(halves):
        for b in range(lc):
            dp_copy(c, b).wait_send()
            pg_copy(c, b).wait_send()

    @pl.loop(0, heads)
    def _(h):
        for s in range(lc):
            ds_copy(h, s).wait_send()


def shards(
    n, nh, query, keys, values, d_gated, tokens, projections, pair_bias, pair, bias_weight,
    atom_mask, token_offsets,
):
    heads, hd, t = query.shape[1:]
    d = tokens.shape[2]
    lc, lh = n.bit_length() - 1, nh.bit_length() - 1
    rows = 4 * heads * hd
    tr, j = t // nh, t // n
    sr = -(-rows // (n * 16)) * 16
    channels = bias_weight.shape[0]
    wide = -(-BINS // 128) * 128
    halves = 2
    dh = d // halves
    args = (
        token_offsets, query[0], keys[0], values[0], d_gated[0], tokens[0],
        projections.reshape(rows, d), pair_bias, pair, bias_weight, atom_mask.reshape(1, t),
        token_offsets.reshape(1, t),
    )

    def vmem():
        return pl.BlockSpec(memory_space=pltpu.VMEM)

    hbm = pl.BlockSpec(memory_space=pltpu.HBM)
    dma = pltpu.SemaphoreType.DMA
    heads_all = nh * heads
    sums = (heads_all, channels + wide)
    d_tokens, d_proj, d_pair, summed = pl.pallas_call(
        functools.partial(main_kernel, n, nh, 1.0 / math.sqrt(hd)),
        out_shape=(
            jax.ShapeDtypeStruct((tr, d), BF16),
            jax.ShapeDtypeStruct((rows, d), BF16),
            jax.ShapeDtypeStruct((tr, j, channels), BF16),
            jax.ShapeDtypeStruct(sums, F32),
        ),
        in_specs=[pl.BlockSpec(memory_space=pltpu.SMEM)] + [hbm] * 8 + [vmem()] * 3,
        out_specs=(vmem(),) * 4,
        scratch_shapes=[
            pltpu.VMEM((heads, hd, t), BF16),
            pltpu.VMEM((heads, hd, t), BF16),
            pltpu.VMEM((heads, hd, t), BF16),
            pltpu.VMEM((heads, hd, t), BF16),
            pltpu.VMEM((rows, d), BF16),
            pltpu.VMEM((heads, t, t), BF16),
            pltpu.VMEM((tr, j, channels), BF16),
            pltpu.VMEM((t, wide), F32),
            pltpu.VMEM((t, wide), F32),
            pltpu.VMEM((2,) * lh + (tr, d), BF16),
            pltpu.VMEM((heads, t, t), BF16),
            pltpu.VMEM((heads, hd, t), F32),
            pltpu.VMEM((t, t), BF16),
            pltpu.VMEM((heads,) + (2,) * lc + (j, t), BF16),
            pltpu.VMEM((4, heads, hd, t), BF16),
            pltpu.VMEM((2,) * lh + (tr, d), BF16),
            pltpu.VMEM((nh, heads, j, tr), BF16),
            pltpu.VMEM((nh, heads, j, tr), BF16),
            pltpu.VMEM((tr, heads_all, j), F32),
            pltpu.VMEM((n,) + sums, F32),
            pltpu.VMEM((nh,) + sums, F32),
            [pltpu.VMEM((2,) * lc + (sr, dh), BF16) for c in range(halves)],
            [pltpu.VMEM((2,) * lc + (sr, dh), BF16) for c in range(halves)],
            [pltpu.VMEM((heads,) + (2,) * (lc - s - 1) + (j, t), BF16) for s in range(lc)],
            [
                [pltpu.VMEM((2,) * (lc - s - 1) + (sr, dh), BF16) for s in range(lc)]
                for c in range(halves)
            ],
            [pltpu.VMEM((2,) * (lh - s - 1) + (tr, d), BF16) for s in range(lh)],
            dma((8,)), dma((2, lh)), dma((2, heads, lc)), dma((2, halves, lc)),
            dma((2, halves, lc)), dma((2, lh)), dma((2, nh)), dma((2, n)), dma((2, nh)),
        ],
        compiler_params=pltpu.CompilerParams(
            collective_id=0, has_side_effects=True, vmem_limit_bytes=50 * 2**20
        ),
    )(*args)
    return (
        d_tokens[None],
        d_proj.astype(F32).reshape(projections.shape),
        d_pair,
        summed[:, :channels].T,
        summed[:, channels : channels + BINS],
    )


def solution(mesh):
    in_specs = (
        P("copy", "head", None, None),
        P("copy", "head", None, None),
        P("copy", "head", None, None),
        P("copy", "head", None, None),
        P("copy", "head", None),
        P(None, "head", None, None),
        P("head", None, None),
        P("head", "copy", None),
        P(),
        P(),
        P(),
    )
    out_specs = (
        P("copy", "head", None),
        P(None, "head", None, None),
        P("head", "copy", None),
        P(),
        P(),
    )
    body = functools.partial(shards, mesh.shape["copy"], mesh.shape["head"])
    return jax.shard_map(body, mesh=mesh, in_specs=in_specs, out_specs=out_specs, check_vma=False)
```

```python
import functools
import math

import jax
import jax.numpy as jnp
from jax import lax
from jax.experimental import pallas as pl
from jax.experimental.pallas import tpu as pltpu
from jax.sharding import PartitionSpec as P

BINS = 65
MASKED_SCORE = -1000000000.0
MESH = pl.DeviceIdType.MESH
F32 = jnp.float32
BF16 = jnp.bfloat16


def contract(a, b, da, db):
    return lax.dot_general(a, b, (((da,), (db,)), ((), ())), preferred_element_type=F32)


def bit_of(index, b):
    return (index // (1 << b)) % 2


def flip(index, b):
    return index + (1 - 2 * bit_of(index, b)) * (1 << b)


def rest(count):
    return (slice(None),) * count


def main_kernel(
    n, nh, scale,
    off_ref, q_hbm, k_hbm, v_hbm, dg_hbm, own_hbm, proj_hbm, bias_hbm, pair_hbm, bw_ref, mask_ref,
    offrow_ref,
    dtok_out, dproj_out, dpair_out, sums_out,
    q_ref, k_ref, v_ref, dg_ref, proj_ref, bias_ref, pair_ref,
    valid_s, off_s, tok, bt, gate, w_s, ds, cot, dt, sb, rb, xs, first, second, dp, pg, rs, ps, ts,
    in_sem, tok_sem, ds_sem, dp_sem, pg_sem, dt_sem, sb_sem, first_sem, second_sem,
):
    lc, lh = n.bit_length() - 1, nh.bit_length() - 1
    heads, hd, t = q_ref.shape
    d = own_hbm.shape[1]
    rows = 4 * heads * hd
    tr = t // nh
    j = t // n
    halves = len(dp)
    dh = d // halves
    copy = lax.axis_index("copy")
    head = lax.axis_index("head")
    cb = [bit_of(copy, b) for b in range(lc)]
    hb = [bit_of(head, b) for b in range(lh)]
    up_order = tuple(range(lc))
    orders = (up_order[1:] + up_order[:1], up_order)

    barrier = pltpu.get_barrier_semaphore()
    for step in range(1, n):
        pl.semaphore_signal(
            barrier, inc=1, device_id={"copy": (copy + step) % n}, device_id_type=MESH
        )
    for step in range(1, nh):
        pl.semaphore_signal(
            barrier, inc=1, device_id={"head": (head + step) % nh}, device_id_type=MESH
        )
    own_index = tuple(hb[b] for b in reversed(range(lh)))
    loads = [
        pltpu.make_async_copy(src, dst, in_sem.at[index])
        for index, (src, dst) in enumerate((
            (own_hbm, tok.at[own_index]), (bias_hbm, bias_ref), (proj_hbm, proj_ref),
            (q_hbm, q_ref), (k_hbm, k_ref), (v_hbm, v_ref), (dg_hbm, dg_ref),
            (pair_hbm, pair_ref),
        ))
    ]
    for load in loads:
        load.start()

    def remote(src, dst, sems, index, device):
        return pltpu.make_async_remote_copy(
            src_ref=src,
            dst_ref=dst,
            send_sem=sems.at[(0,) + index],
            recv_sem=sems.at[(1,) + index],
            device_id=device,
            device_id_type=MESH,
        )

    def pick(order, bits, s, other):
        left = sorted(order[s:], reverse=True)
        bit = bits[order[s]]
        return rest(left.index(order[s])) + ((1 - bit if other else bit),)

    def halve(src, dst, order, bits, s, sems, index, device, lead=()):
        to = dst.at[lead] if lead else dst
        return remote(src.at[lead + pick(order, bits, s, True)], to, sems, index, device)

    def fold(src, dst, order, bits, s, lead=()):
        whole = lead if lead else Ellipsis
        mine = src[lead + pick(order, bits, s, False)]
        dst[whole] = (mine.astype(F32) + dst[whole].astype(F32)).astype(BF16)

    def spread(ref, order, bits, s, sems, index, device):
        done = order[s + 1 :]
        at = tuple(
            slice(None) if b in done else bits[b] for b in reversed(range(len(bits)))
        )
        return remote(ref.at[at], ref.at[at], sems, index, device)

    def tok_copy(b):
        return spread(tok, tuple(range(lh)), hb, b, tok_sem, (b,), {"head": flip(head, b)})

    def ds_copy(h, s):
        src = ds if s == 0 else rs[s - 1]
        return halve(
            src, rs[s], up_order, cb, s, ds_sem, (h, s), {"copy": flip(copy, s)}, (h,)
        )

    def dp_copy(c, s):
        src = dp[c] if s == 0 else ps[c][s - 1]
        device = {"copy": flip(copy, orders[c][s])}
        return halve(src, ps[c][s], orders[c], cb, s, dp_sem, (c, s), device)

    def pg_copy(c, s):
        device = {"copy": flip(copy, orders[c][s])}
        return spread(pg[c], orders[c], cb, s, pg_sem, (c, s), device)

    def dt_copy(s):
        src = dt if s == 0 else ts[s - 1]
        return halve(
            src, ts[s], tuple(range(lh)), hb, s, dt_sem, (s,), {"head": flip(head, s)}
        )

    def sb_copy(step):
        peer = (head + step) % nh
        return remote(sb.at[peer], rb.at[head], sb_sem, (step,), {"head": peer})

    def first_copy(step):
        here = first.at[copy]
        return remote(here, here, first_sem, (step,), {"copy": (copy + step) % n})

    def second_copy(step):
        here = second.at[head]
        return remote(here, here, second_sem, (step,), {"head": (head + step) % nh})

    loads[0].wait()
    pl.semaphore_wait(barrier, n + nh - 2)
    tok_copy(lh - 1).start()
    wide = valid_s.shape[1]
    valid_s[...] = jnp.broadcast_to(mask_ref[...].astype(F32), (wide, t)).T
    off_s[...] = jnp.broadcast_to(offrow_ref[...].astype(F32), (wide, t)).T
    loads[1].wait()

    @pl.loop(0, heads)
    def _(h):
        bt[h] = bias_ref[h].T

    for b in reversed(range(lh)):
        tok_copy(b).wait_recv()
        if b > 0:
            tok_copy(b - 1).start()
    for load in loads[2:]:
        load.wait()
    tokens = tok[...].reshape(t, d)
    gate_pre = contract(proj_ref[3 * heads * hd :, :], tokens, 1, 1)
    gate[...] = jax.nn.sigmoid(gate_pre).reshape(heads, hd, t)

    ib = min(t, 256)

    def compute(h):
        valid = valid_s[:, 0:1] > 0.5
        keys, values = k_ref[h], v_ref[h]
        for start in range(0, t, ib):
            cols = pl.ds(start, ib)
            query = q_ref[h, :, cols]
            s = contract(keys, query, 0, 0) * scale + bt[h, :, cols].astype(F32)
            s = jnp.where(valid, s, MASKED_SCORE)
            e = jnp.exp(s - jnp.max(s, axis=0, keepdims=True))
            p = e * (1.0 / jnp.sum(e, axis=0, keepdims=True))
            w = p.astype(BF16)
            w_s[:, cols] = w
            att = contract(values, w, 1, 0)
            g = gate[h, :, cols]
            up = dg_ref[h, :, cols].astype(F32)
            datt = (up * g).astype(BF16)
            cot[2, h, :, cols] = datt
            cot[3, h, :, cols] = (up * att * g * (1.0 - g)).astype(BF16)
            inner = jnp.sum(datt.astype(F32) * att, axis=0, keepdims=True)
            dprob = contract(values, datt, 0, 0)
            dsb = (p * (dprob - inner)).astype(BF16)
            ds[(h,) + rest(lc + 1) + (cols,)] = dsb.reshape((2,) * lc + (j, ib))
            cot[0, h, :, cols] = (contract(keys, dsb, 1, 0) * scale).astype(BF16)

    def finish(h):
        full = ds[h].reshape(t, t)
        cot[1, h] = (contract(q_ref[h], full, 1, 1) * scale).astype(BF16)
        cot[2, h] = contract(cot[2, h], w_s[...], 1, 1).astype(BF16)

    lag = 1

    def advance(h, s):
        ds_copy(h, s - 1).wait_recv()
        fold(ds if s == 1 else rs[s - 2], rs[s - 1], up_order, cb, s - 1, (h,))
        if s < lc:
            ds_copy(h, s).start()

    @pl.loop(0, heads)
    def _(h):
        compute(h)
        ds_copy(h, 0).start()
        finish(h)
        for s in range(1, lc + 1):

            @pl.when(h >= s + lag)
            def _():
                advance(h - s - lag, s)

    def drain(now):
        for s in range(1, lc + 1):
            if 0 <= now - s - lag < heads:
                advance(now - s - lag, s)

    def dp_advance(c, s):
        dp_copy(c, s - 1).wait_recv()
        fold(dp[c] if s == 1 else ps[c][s - 2], ps[c][s - 1], orders[c], cb, s - 1)
        if s < lc:
            dp_copy(c, s).start()

    def dt_advance(s):
        dt_copy(s - 1).wait_recv()
        fold(dt if s == 1 else ts[s - 2], ts[s - 1], tuple(range(lh)), hb, s - 1)
        if s < lh:
            dt_copy(s).start()

    flat = cot[...].reshape(rows, t)
    sr = dp[0].shape[-2]
    for c in range(halves):
        tokens = tok[...].reshape(t, d)[:, c * dh : (c + 1) * dh]
        part = contract(flat, tokens, 1, 0).astype(BF16)
        if rows < n * sr:
            part = jnp.concatenate([part, jnp.zeros((n * sr - rows, dh), BF16)], axis=0)
        dp[c][...] = part.reshape((2,) * lc + (sr, dh))
        dp_copy(c, 0).start()
    drain(heads)
    dt[...] = contract(flat, proj_ref[...], 0, 0).astype(BF16).reshape((2,) * lh + (tr, d))
    dt_copy(0).start()
    drain(heads + 1)
    dp_advance(0, 1)
    for now in range(heads + 2, heads + lc + lag):
        drain(now)

    total = rs[lc - 1]
    for peer in range(nh):
        sb[peer] = total[:, :, peer * tr : (peer + 1) * tr]
    for step in range(1, nh):
        sb_copy(step).start()
    rb[head] = sb[head]

    dt_advance(1)
    dp_advance(1, 1)
    dp_advance(0, 2)
    for step in range(1, nh):
        sb_copy(step).wait()
    for peer in range(nh):
        for h in range(heads):
            xs[:, peer * heads + h, :] = rb[peer, h].astype(F32).T
    columns = off_s[pl.ds(pl.multiple_of(copy * j, j), j), :]
    bins = lax.broadcasted_iota(jnp.int32, (j, wide), 1).astype(F32)
    reach = (BINS - 1) // 2
    group = 8
    channels = bw_ref.shape[0]

    def pairs(g, acc):
        for u in range(group):
            i = g * group + u
            x = xs[i].astype(BF16)
            dpair_out[i] = contract(x, bw_ref[...], 0, 1).astype(BF16)
            gap = columns - off_ref[head * tr + i].astype(F32)
            hot = jnp.clip(gap, -reach, reach) + reach == bins
            right = jnp.concatenate([pair_ref[i], hot.astype(F32).astype(BF16)], axis=1)
            acc = acc + contract(x, right, 1, 0)
        return acc

    acc = jnp.zeros((nh * heads, channels + wide), F32)
    acc = lax.fori_loop(0, tr // group // 2, pairs, acc)
    for s in range(2, lc):
        if s <= lh:
            dt_advance(s)
        dp_advance(1, s)
        dp_advance(0, s + 1)
    for s in range(lc, lh + 1):
        dt_advance(s)
    dtok_out[...] = ts[lh - 1][...]
    mine = tuple(cb[b] for b in reversed(range(lc)))
    pg[0][mine] = ps[0][lc - 1][...]
    pg_copy(0, lc - 1).start()
    acc = lax.fori_loop(tr // group // 2, tr // group, pairs, acc)
    first[copy] = acc
    for step in range(1, n):
        first_copy(step).start()
    dp_advance(1, lc)
    pg[1][mine] = ps[1][lc - 1][...]
    pg_copy(1, lc - 1).start()

    def pg_advance(s):
        for c in range(halves):
            pg_copy(c, s).wait_recv()
            if s > 0:
                pg_copy(c, s - 1).start()

    pg_advance(lc - 1)
    for step in range(1, n):
        first_copy(step).wait()
    acc = first[0]
    for index in range(1, n):
        acc = acc + first[index]
    second[head] = acc
    for step in range(1, nh):
        second_copy(step).start()
    for s in reversed(range(lc - 1)):
        pg_advance(s)
    for c in range(halves):
        dproj_out[:, c * dh : (c + 1) * dh] = pg[c][...].reshape(n * sr, dh)[:rows]
    for step in range(1, nh):
        second_copy(step).wait()
    acc = second[0]
    for index in range(1, nh):
        acc = acc + second[index]
    sums_out[...] = acc
    for b in range(lh):
        tok_copy(b).wait_send()
        dt_copy(b).wait_send()
    for c in range(halves):
        for b in range(lc):
            dp_copy(c, b).wait_send()
            pg_copy(c, b).wait_send()

    @pl.loop(0, heads)
    def _(h):
        for s in range(lc):
            ds_copy(h, s).wait_send()


def shards(
    n, nh, query, keys, values, d_gated, tokens, projections, pair_bias, pair, bias_weight,
    atom_mask, token_offsets,
):
    heads, hd, t = query.shape[1:]
    d = tokens.shape[2]
    lc, lh = n.bit_length() - 1, nh.bit_length() - 1
    rows = 4 * heads * hd
    tr, j = t // nh, t // n
    sr = -(-rows // (n * 16)) * 16
    channels = bias_weight.shape[0]
    wide = -(-BINS // 128) * 128
    halves = 2
    dh = d // halves
    args = (
        token_offsets, query[0], keys[0], values[0], d_gated[0], tokens[0],
        projections.reshape(rows, d), pair_bias, pair, bias_weight, atom_mask.reshape(1, t),
        token_offsets.reshape(1, t),
    )

    def vmem():
        return pl.BlockSpec(memory_space=pltpu.VMEM)

    hbm = pl.BlockSpec(memory_space=pltpu.HBM)
    dma = pltpu.SemaphoreType.DMA
    heads_all = nh * heads
    sums = (heads_all, channels + wide)
    d_tokens, d_proj, d_pair, summed = pl.pallas_call(
        functools.partial(main_kernel, n, nh, 1.0 / math.sqrt(hd)),
        out_shape=(
            jax.ShapeDtypeStruct((tr, d), BF16),
            jax.ShapeDtypeStruct((rows, d), BF16),
            jax.ShapeDtypeStruct((tr, j, channels), BF16),
            jax.ShapeDtypeStruct(sums, F32),
        ),
        in_specs=[pl.BlockSpec(memory_space=pltpu.SMEM)] + [hbm] * 8 + [vmem()] * 3,
        out_specs=(vmem(),) * 4,
        scratch_shapes=[
            pltpu.VMEM((heads, hd, t), BF16),
            pltpu.VMEM((heads, hd, t), BF16),
            pltpu.VMEM((heads, hd, t), BF16),
            pltpu.VMEM((heads, hd, t), BF16),
            pltpu.VMEM((rows, d), BF16),
            pltpu.VMEM((heads, t, t), BF16),
            pltpu.VMEM((tr, j, channels), BF16),
            pltpu.VMEM((t, wide), F32),
            pltpu.VMEM((t, wide), F32),
            pltpu.VMEM((2,) * lh + (tr, d), BF16),
            pltpu.VMEM((heads, t, t), BF16),
            pltpu.VMEM((heads, hd, t), F32),
            pltpu.VMEM((t, t), BF16),
            pltpu.VMEM((heads,) + (2,) * lc + (j, t), BF16),
            pltpu.VMEM((4, heads, hd, t), BF16),
            pltpu.VMEM((2,) * lh + (tr, d), BF16),
            pltpu.VMEM((nh, heads, j, tr), BF16),
            pltpu.VMEM((nh, heads, j, tr), BF16),
            pltpu.VMEM((tr, heads_all, j), F32),
            pltpu.VMEM((n,) + sums, F32),
            pltpu.VMEM((nh,) + sums, F32),
            [pltpu.VMEM((2,) * lc + (sr, dh), BF16) for c in range(halves)],
            [pltpu.VMEM((2,) * lc + (sr, dh), BF16) for c in range(halves)],
            [pltpu.VMEM((heads,) + (2,) * (lc - s - 1) + (j, t), BF16) for s in range(lc)],
            [
                [pltpu.VMEM((2,) * (lc - s - 1) + (sr, dh), BF16) for s in range(lc)]
                for c in range(halves)
            ],
            [pltpu.VMEM((2,) * (lh - s - 1) + (tr, d), BF16) for s in range(lh)],
            dma((8,)), dma((2, lh)), dma((2, heads, lc)), dma((2, halves, lc)),
            dma((2, halves, lc)), dma((2, lh)), dma((2, nh)), dma((2, n)), dma((2, nh)),
        ],
        compiler_params=pltpu.CompilerParams(
            collective_id=0, has_side_effects=True, vmem_limit_bytes=62 * 2**20
        ),
    )(*args)
    return (
        d_tokens[None],
        d_proj.astype(F32).reshape(projections.shape),
        d_pair,
        summed[:, :channels].T,
        summed[:, channels : channels + BINS],
    )


def solution(mesh):
    in_specs = (
        P("copy", "head", None, None),
        P("copy", "head", None, None),
        P("copy", "head", None, None),
        P("copy", "head", None, None),
        P("copy", "head", None),
        P(None, "head", None, None),
        P("head", None, None),
        P("head", "copy", None),
        P(),
        P(),
        P(),
    )
    out_specs = (
        P("copy", "head", None),
        P(None, "head", None, None),
        P("head", "copy", None),
        P(),
        P(),
    )
    body = functools.partial(shards, mesh.shape["copy"], mesh.shape["head"])
    return jax.shard_map(body, mesh=mesh, in_specs=in_specs, out_specs=out_specs, check_vma=False)
```
